32 devices in a mesh: expert: 16 (over z, y, x), dp: 2 (over core).
Axes of the slice: x: 2, y: 2, z: 4, core: 2. Of those that a mesh axis runs over, the one named last changes fastest.
Arguments:
- tokens: bfloat16 [768, 2048], P(('expert', 'dp')), may hold values from -6 to 6
- expert_ids: int32 [768, 8], P(('expert', 'dp')), may hold values from 0 to 15, all different within a row; in each aligned block of 24 rows (0 to 23, 24 to 47, ...) at most 16 rows name the same one
- route_weight: float32 [768, 8], P(('expert', 'dp')), may hold values from 0.05 to 0.5
- cotangent: bfloat16 [768, 2048], P(('expert', 'dp')), may hold values from -6 to 6
- holder: int32 [16], replicated, may hold values from 0 to 15, each once
- partner: int32 [16], replicated, may hold values from 0 to 15, as said below
- up_weight: bfloat16 [16, 2048, 768], P('expert', 'dp'), may hold values from -0.125 to 0.125
- down_weight: bfloat16 [16, 768, 2048], P('expert', None, 'dp'), may hold values from -0.21875 to 0.21875
- up_moment: bfloat16 [16, 2048, 768], P('expert', 'dp'), may hold values from -1.796875 to 1.796875
- down_moment: bfloat16 [16, 768, 2048], P('expert', None, 'dp'), may hold values from -1.796875 to 1.796875
Outputs:
- layer_out: bfloat16 [768, 2048], P(('expert', 'dp'))
- up_moment_new: bfloat16 [16, 2048, 768], P('expert', 'dp')
- down_moment_new: bfloat16 [16, 768, 2048], P('expert', None, 'dp')
The draws below stay inside these ranges and needn't reach their ends.
Inputs may be any that keep to these rules, and one draw needn't show every extreme that they name: `expert_ids`: each token names 8 different experts; within each device's block of 24 tokens no expert is named by more than 16 tokens, a bound that some block reaches. `holder`: A permutation of the slots. partner[partner[s]] = s for every slot s, and exactly 2 * (4) slots have partner[s] != s.
All inputs are finite; a program needn't handle non-finite values.
Results may differ from the reference program's by a relative error of at most 0.022.
Values may be sent and summed in bfloat16 or wider, within the bound.
A program may use at most 128 MiB of HBM per device.

```python
import math
import jax
import jax.numpy as jnp
import numpy as np
from jax import lax

D = 2048
F = 768
TOPK = 8
TOK_DEV = 24
EXPERTS = 16
CAP = 16
TOKENS = 768
N_DP = 2


def draw_partner(key, part):
    order = jax.random.permutation(key, EXPERTS).astype(jnp.int32)
    pairs = EXPERTS // 4
    first = order[0:2 * pairs:2]
    second = order[1:2 * pairs:2]
    base = jnp.arange(EXPERTS, dtype=jnp.int32)
    return base.at[first].set(second).at[second].set(first)


def block_scale(rng, extent, split, low, largest):
    def one(axis_at, shards_of):
        heights = jax.random.uniform(jax.random.fold_in(jax.random.fold_in(rng, 6), axis_at), (shards_of,), jnp.float32, low / len(split), largest / len(split))
        return jnp.repeat(jnp.exp(heights), extent[axis_at] // shards_of).reshape((-1,) + (1,) * (len(extent) - axis_at - 1))

    gain = one(*split[0])
    for cut in split[1:]:
        gain = gain * one(*cut)
    return gain


def shared_out(own_key, own, number, rows, number_of, top, limit, skew):
    order = jax.random.permutation(own_key, number_of)
    packed, usual = shares(number_of, rows * top, limit, skew, True), shares(number_of, rows * top, limit, skew, False)
    places = jnp.arange(number_of)

    def named(lengths, turn):
        used = int((lengths > 0).sum())
        fixed = max(1, used // 4)
        shifted = fixed + (places - fixed + turn * (used - fixed)) % max(1, number_of - fixed)
        return jnp.zeros((number_of,), jnp.int32).at[order[jnp.where(places < fixed, places, shifted)]].set(jnp.asarray(lengths, jnp.int32))

    lengths = jnp.where(number % 4 == 0, named(packed, number // 4), named(usual, number - number // 4 - 1))
    mixed = jax.random.permutation(jax.random.fold_in(own, 3), number_of)
    donor, taker = mixed[0:number_of // 2 * 2:2], mixed[1:number_of // 2 * 2:2]
    margin = jnp.minimum(lengths[donor] - 1, limit - lengths[taker]) // 2
    margin = jnp.where((donor == order[0]) | (taker == order[0]) | (lengths[taker] == 0), 0, jnp.maximum(margin, 0))
    shifted = jax.random.randint(jax.random.fold_in(own, 4), (number_of // 2,), 0, 1 << 20) % (margin + 1)
    lengths = lengths.at[donor].add(-shifted).at[taker].add(shifted)
    labels = jnp.searchsorted(jnp.cumsum(lengths), jnp.arange(rows * top), side="right").astype(jnp.int32)
    grid = labels.reshape(top, rows).T
    grid = grid[jax.random.permutation(jax.random.fold_in(own, 1), rows)]
    turn = jax.random.randint(jax.random.fold_in(own, 2), (rows, 1), 0, top)
    return jnp.take_along_axis(grid, (jnp.arange(top)[None, :] + turn) % top, axis=1)


def shares(amount, total, bound, lean, full):
    loads = [(1 << 20) // math.isqrt(rank ** lean) + 1 for rank in range(1, amount + 1)]
    largest = bound if full else min(bound, max(-(-total // amount), total * loads[0] // sum(loads)))
    least = 1 if total - largest >= amount - 1 else 0
    counts, spare = [largest] + [least] * (amount - 1), total - largest - least * (amount - 1)
    while spare > 0:
        movable = [i for i in range(1, amount) if counts[i] < largest] or [i for i in range(1, amount) if counts[i] < bound]
        pool, remaining = sum([loads[i] for i in movable]), spare
        for i in movable:
            addition = min(bound - counts[i], max(1, remaining * loads[i] // pool), spare)
            counts[i] = counts[i] + addition
            spare = spare - addition
    return np.array(counts)


def normal_values(stream_key, shape, scale, bound, pieces=(), held_as=jnp.bfloat16):
    drawn = jax.random.normal(stream_key, shape, jnp.float32) * scale
    if len(pieces) > 0:
        drawn = block_scale(stream_key, shape, pieces, -0.22, 0.18) * drawn
    return jnp.clip(drawn, min=-bound, max=bound).astype(held_as)


def setup_inputs(seed: int = 0) -> dict:
    keys = jax.random.split(jax.random.key(seed), 11)
    tokens = normal_values(keys[0], (TOKENS, D), 1.0, 6.0, ((0, 32),))
    expert_ids_keys = jax.random.split(jax.random.fold_in(keys[1], 1), TOKENS // TOK_DEV)
    expert_ids_turns = jax.random.permutation(jax.random.fold_in(keys[1], 3), TOKENS // TOK_DEV)
    expert_ids = jax.vmap(lambda own, number: shared_out(jax.random.fold_in(keys[1], 2), own, number, TOK_DEV, EXPERTS, TOPK, CAP, 2))(expert_ids_keys, expert_ids_turns).reshape((TOKENS, TOPK))
    route_weight = jnp.clip(jnp.exp(math.log(0.5) - 2.3025851 * jax.random.uniform(keys[2], (TOKENS, TOPK), jnp.float32) ** block_scale(keys[2], (TOKENS, TOPK), ((0, 32),), -0.2, 0.2)), 0.05, 0.5)
    cotangent = normal_values(keys[3], (TOKENS, D), 1.0, 6.0, ((0, 32),))
    holder = jax.random.permutation(keys[4], EXPERTS).astype(jnp.int32)
    partner = draw_partner(jax.random.fold_in(keys[10], 71), 0)
    up_weight = normal_values(keys[6], (EXPERTS, D, F), D ** -0.5, 0.125, ((0, 16), (1, 2)))
    down_weight = normal_values(keys[7], (EXPERTS, F, D), F ** -0.5, 0.21875, ((0, 16), (2, 2)))
    up_moment = normal_values(keys[8], (EXPERTS, D, F), 0.3, 1.796875, ((0, 16), (1, 2)))
    down_moment = normal_values(keys[9], (EXPERTS, F, D), 0.3, 1.796875, ((0, 16), (2, 2)))
    return {"tokens": tokens, "expert_ids": expert_ids, "route_weight": route_weight, "cotangent": cotangent, "holder": holder, "partner": partner, "up_weight": up_weight, "down_weight": down_weight, "up_moment": up_moment, "down_moment": down_moment}


MOMENT_DECAY = 0.9


def silu_slope(preact):
    sigmoid_value = jax.nn.sigmoid(preact)
    return sigmoid_value * (1.0 + preact * (1.0 - sigmoid_value))


def reference(tokens, expert_ids, route_weight, cotangent, holder, partner, up_weight, down_weight, up_moment, down_moment):
    blocks = TOKENS // TOK_DEV
    per_block = TOK_DEV * TOPK
    quarter = D // N_DP
    expert_rows = expert_ids.reshape(blocks, per_block)
    experts = jnp.arange(EXPERTS, dtype=jnp.int32)
    hit_table = (expert_rows[:, :, None] == experts[None, None, :]).astype(jnp.int32)
    position = jnp.sum((jnp.cumsum(hit_table, axis=1) - 1) * hit_table, axis=2)
    block_index = jnp.arange(blocks, dtype=jnp.int32)[:, None]
    entry_index = ((expert_rows * blocks + block_index) * CAP + position).reshape(-1).astype(jnp.int32)
    token_index = (block_index * TOK_DEV + jnp.arange(per_block, dtype=jnp.int32)[None, :] // TOPK).reshape(-1).astype(jnp.int32)
    slot_span = blocks * CAP
    token_table = jnp.full((EXPERTS * slot_span,), TOKENS, dtype=jnp.int32).at[entry_index].set(token_index)
    weights = jnp.zeros((EXPERTS * slot_span,), jnp.float32).at[entry_index].set(route_weight.reshape(-1))
    padded_tokens = jnp.concatenate([tokens, jnp.zeros((1, D), tokens.dtype)], axis=0)
    padded_grads = jnp.concatenate([cotangent.astype(jnp.float32), jnp.zeros((1, D), jnp.float32)], axis=0)

    def one_expert(accumulated, expert):
        row_index = lax.dynamic_slice_in_dim(token_table, expert * slot_span, slot_span)
        scales = lax.dynamic_slice_in_dim(weights, expert * slot_span, slot_span)
        inputs = padded_tokens[row_index]
        cotangents = (scales[:, None] * padded_grads[row_index]).astype(jnp.bfloat16)
        old_slot = holder[expert]
        w_up = up_weight[old_slot]
        w_down = down_weight[old_slot]
        preact = jnp.zeros((slot_span, F), jnp.float32)
        back_sum = jnp.zeros((slot_span, F), jnp.float32)
        for section in range(N_DP):
            begin_at = section * quarter
            end_at = begin_at + quarter
            part_up = jnp.dot(inputs[:, begin_at:end_at], w_up[begin_at:end_at, :], preferred_element_type=jnp.float32)
            preact = preact + lax.optimization_barrier(part_up.astype(jnp.bfloat16)).astype(jnp.float32)
            part_back = jnp.dot(cotangents[:, begin_at:end_at], w_down[:, begin_at:end_at].T, preferred_element_type=jnp.float32)
            back_sum = back_sum + lax.optimization_barrier(part_back.astype(jnp.bfloat16)).astype(jnp.float32)
        hidden = jax.nn.silu(preact).astype(jnp.bfloat16)
        pre_grad = (back_sum * silu_slope(preact)).astype(jnp.bfloat16)
        outputs = jnp.dot(hidden, w_down, preferred_element_type=jnp.float32).astype(jnp.bfloat16)
        up_grad = jnp.dot(inputs.T, pre_grad, preferred_element_type=jnp.float32)
        down_grad = jnp.dot(hidden.T, cotangents, preferred_element_type=jnp.float32)
        new_up = (MOMENT_DECAY * up_moment[old_slot].astype(jnp.float32) + (1.0 - MOMENT_DECAY) * up_grad).astype(jnp.bfloat16)
        new_down = (MOMENT_DECAY * down_moment[old_slot].astype(jnp.float32) + (1.0 - MOMENT_DECAY) * down_grad).astype(jnp.bfloat16)
        accumulated = accumulated.at[row_index].add(scales[:, None] * outputs.astype(jnp.float32))
        return accumulated, (new_up, new_down)

    start = jnp.zeros((TOKENS + 1, D), jnp.float32)
    accumulated, stacked = lax.scan(one_expert, start, experts)
    inverse = jnp.zeros((EXPERTS,), jnp.int32).at[holder].set(experts)
    order = inverse[partner]
    return accumulated[:TOKENS].astype(jnp.bfloat16), stacked[0][order], stacked[1][order]
```

```python
import jax
import jax.numpy as jnp
from jax import lax
from jax.sharding import PartitionSpec as P

MOMENT_DECAY = 0.9


def silu_slope(preact):
    sigmoid_value = jax.nn.sigmoid(preact)
    return sigmoid_value * (1.0 + preact * (1.0 - sigmoid_value))


def swap_slots(arrays, partner, slot_count):
    stacked = jnp.stack([array_item.reshape(slot_count, -1) for array_item in arrays], axis=1)
    spread = lax.all_to_all(stacked, "expert", split_axis=0, concat_axis=0, tiled=True)
    picked = jnp.take(spread, partner, axis=0)
    landed = lax.all_to_all(picked, "expert", split_axis=0, concat_axis=0, tiled=True)
    return [landed[:, member].reshape(array_item.shape) for member, array_item in enumerate(arrays)]


def body(
    tokens,
    expert_ids,
    route_weight,
    cotangent,
    holder,
    partner,
    up_weight,
    down_weight,
    up_moment,
    down_moment,
):
    tok_count, top_count = expert_ids.shape
    n_slots = lax.axis_size("expert")
    n_groups = lax.axis_size("dp")
    capacity = min(tok_count, max(2, 4 * tok_count * top_count // (3 * n_slots)))
    feature_count = tokens.shape[1]
    quarter = feature_count // n_groups
    slot_range = jnp.arange(n_slots, dtype=jnp.int32)
    held_hit = (holder[:, None] == slot_range[None, :]).astype(jnp.int32)
    target = jnp.sum(held_hit * partner[None, :], axis=1)
    swapped = swap_slots([up_weight, down_weight, up_moment, down_moment], partner, n_slots)
    up_weight, down_weight, up_moment, down_moment = (
        swapped[0],
        swapped[1],
        swapped[2],
        swapped[3],
    )
    flat_ids = expert_ids.reshape(-1)
    expert_hit = (flat_ids[:, None] == slot_range[None, :]).astype(jnp.int32)
    destination = jnp.sum(expert_hit * target[None, :], axis=1)
    dest_hit = (destination[:, None] == slot_range[None, :]).astype(jnp.int32)
    position = jnp.sum((jnp.cumsum(dest_hit, axis=0) - 1) * dest_hit, axis=1)
    entry_index = destination * capacity + position
    slots_total = n_slots * capacity
    select = (jnp.arange(slots_total, dtype=jnp.int32)[:, None] == entry_index[None, :]).reshape(
        slots_total, tok_count, top_count
    )
    picked = jnp.sum(select.astype(jnp.float32), axis=2)
    scaled = jnp.sum(jnp.where(select, route_weight[None, :, :], 0.0), axis=2)
    sent_rows = jnp.dot(
        picked.astype(jnp.bfloat16), tokens, preferred_element_type=jnp.float32
    ).astype(jnp.bfloat16)
    sent_grads = jnp.dot(
        scaled,
        cotangent.astype(jnp.float32),
        precision=lax.Precision.HIGHEST,
        preferred_element_type=jnp.float32,
    ).astype(jnp.bfloat16)
    outgoing = jnp.stack([sent_rows, sent_grads], axis=0).reshape(
        1, 2, n_slots, capacity, feature_count
    )
    arrived = lax.all_to_all(
        lax.all_to_all(outgoing, "expert", split_axis=2, concat_axis=2, tiled=True),
        "dp",
        split_axis=4,
        concat_axis=0,
        tiled=True,
    )
    rows_in = arrived[:, 0].reshape(-1, quarter)
    grads_in = arrived[:, 1].reshape(-1, quarter)
    up_local = up_weight[0]
    down_local = down_weight[0]
    pre_part = jnp.dot(rows_in, up_local, preferred_element_type=jnp.float32)
    back_part = lax.dot_general(
        grads_in, down_local, (((1,), (1,)), ((), ())), preferred_element_type=jnp.float32
    )
    preact, back_sum = (
        lax.psum(pre_part.astype(jnp.bfloat16), "dp").astype(jnp.float32),
        lax.psum(back_part.astype(jnp.bfloat16), "dp").astype(jnp.float32),
    )
    hidden = jax.nn.silu(preact).astype(jnp.bfloat16)
    pre_grad = (back_sum * silu_slope(preact)).astype(jnp.bfloat16)
    out_part = jnp.dot(hidden, down_local, preferred_element_type=jnp.float32).astype(jnp.bfloat16)
    up_grad = lax.dot_general(
        rows_in, pre_grad, (((0,), (0,)), ((), ())), preferred_element_type=jnp.float32
    )
    down_grad = lax.dot_general(
        hidden, grads_in, (((0,), (0,)), ((), ())), preferred_element_type=jnp.float32
    )
    returned = lax.all_to_all(
        lax.all_to_all(
            out_part.reshape(n_groups, n_slots, capacity, quarter),
            "expert",
            split_axis=1,
            concat_axis=1,
            tiled=True,
        ),
        "dp",
        split_axis=0,
        concat_axis=3,
        tiled=True,
    )
    layer_out = jnp.dot(
        scaled.T,
        returned.reshape(slots_total, feature_count).astype(jnp.float32),
        precision=lax.Precision.HIGHEST,
        preferred_element_type=jnp.float32,
    ).astype(jnp.bfloat16)
    new_up = (
        MOMENT_DECAY * up_moment.astype(jnp.float32) + (1.0 - MOMENT_DECAY) * up_grad[None]
    ).astype(jnp.bfloat16)
    new_down = (
        MOMENT_DECAY * down_moment.astype(jnp.float32) + (1.0 - MOMENT_DECAY) * down_grad[None]
    ).astype(jnp.bfloat16)
    return (layer_out, new_up, new_down)


def own_weights(expert_ids, route_weight, holder, slot_count):
    slot_range = jnp.arange(slot_count, dtype=jnp.int32)
    ids_hit = expert_ids[:, :, None] == slot_range[None, None, :]
    by_expert = jnp.sum(jnp.where(ids_hit, route_weight[:, :, None], 0.0), axis=1)
    placed = holder[:, None] == slot_range[None, :]
    by_slot = jnp.sum(jnp.where(placed[None], by_expert[:, :, None], 0.0), axis=1)
    return by_slot


def move_slots(array_item, partner, slot_count):
    rows, columns = array_item.shape
    pieces = array_item.reshape(slot_count, rows // slot_count, columns)
    spread = lax.all_to_all(pieces, "expert", split_axis=0, concat_axis=0, tiled=True)
    picked = jnp.take(spread, partner, axis=0)
    landed = lax.all_to_all(picked, "expert", split_axis=0, concat_axis=0, tiled=True)
    return landed.reshape(1, rows, columns)


def dense_body(
    tokens,
    expert_ids,
    route_weight,
    cotangent,
    holder,
    partner,
    up_weight,
    down_weight,
    up_moment,
    down_moment,
):
    n_slots = lax.axis_size("expert")
    tok_count, feature_count = tokens.shape
    half = feature_count // 2
    swap_pair = [(0, 1), (1, 0)]
    me = lax.axis_index("expert")
    by_slot = own_weights(expert_ids, route_weight, holder, n_slots)
    gathered_weights = lax.all_gather(by_slot, ("expert", "dp"), axis=0, tiled=True)
    scale = jnp.sum(
        jnp.where(jnp.arange(n_slots)[None, :] == me, gathered_weights, 0.0), axis=1, keepdims=True
    )
    both = lax.all_to_all(
        jnp.stack([tokens, cotangent]), "dp", split_axis=2, concat_axis=1, tiled=True
    )
    every = lax.all_gather(both, "expert", axis=1, tiled=True)
    rows, cots = every[0], every[1]
    grads = (scale * cots.astype(jnp.float32)).astype(jnp.bfloat16)
    up_local, down_local = up_weight[0], down_weight[0]
    pre_part = jnp.dot(rows, up_local, preferred_element_type=jnp.float32).astype(jnp.bfloat16)
    back_part = lax.dot_general(
        grads, down_local, (((1,), (1,)), ((), ())), preferred_element_type=jnp.float32
    ).astype(jnp.bfloat16)
    preact = pre_part.astype(jnp.float32) + lax.ppermute(pre_part, "dp", swap_pair).astype(
        jnp.float32
    )
    back_sum = back_part.astype(jnp.float32) + lax.ppermute(back_part, "dp", swap_pair).astype(
        jnp.float32
    )
    hidden = jax.nn.silu(preact).astype(jnp.bfloat16)
    pre_grad = (back_sum * silu_slope(preact)).astype(jnp.bfloat16)
    up_grad = lax.dot_general(
        rows, pre_grad, (((0,), (0,)), ((), ())), preferred_element_type=jnp.float32
    )
    new_up = (
        MOMENT_DECAY * up_moment[0].astype(jnp.float32) + (1.0 - MOMENT_DECAY) * up_grad
    ).astype(jnp.bfloat16)
    down_grad = lax.dot_general(
        hidden, grads, (((0,), (0,)), ((), ())), preferred_element_type=jnp.float32
    )
    new_down = (
        MOMENT_DECAY * down_moment[0].astype(jnp.float32) + (1.0 - MOMENT_DECAY) * down_grad
    ).astype(jnp.bfloat16)
    out_part = jnp.dot(hidden, down_local, preferred_element_type=jnp.float32).astype(jnp.bfloat16)
    out_part = (scale * out_part.astype(jnp.float32)).astype(jnp.bfloat16)
    moved_up = move_slots(new_up, partner, n_slots)
    moved_down = move_slots(new_down, partner, n_slots)
    parts = lax.all_to_all(
        out_part.reshape(n_slots, 2 * tok_count, half),
        "expert",
        split_axis=0,
        concat_axis=0,
        tiled=True,
    )
    summed = jnp.sum(parts.astype(jnp.float32), axis=0).astype(jnp.bfloat16)
    layer_out = lax.all_to_all(summed, "dp", split_axis=0, concat_axis=1, tiled=True)
    return (layer_out, moved_up, moved_down)


def pick_body(mesh):
    def chosen(tokens, *others):
        dense = mesh.shape["dp"] == 2 and tokens.shape[0] * mesh.size <= 2048
        return (dense_body if dense else body)(tokens, *others)

    return chosen


def solution(mesh):
    return jax.shard_map(
        pick_body(mesh),
        mesh=mesh,
        in_specs=(
            P(("expert", "dp"), None),
            P(("expert", "dp"), None),
            P(("expert", "dp"), None),
            P(("expert", "dp"), None),
            P(),
            P(),
            P("expert", "dp", None),
            P("expert", None, "dp"),
            P("expert", "dp", None),
            P("expert", None, "dp"),
        ),
        out_specs=(P(("expert", "dp"), None), P("expert", "dp", None), P("expert", None, "dp")),
        check_vma=False,
    )
```

```python
import jax
import jax.numpy as jnp
from jax import lax
from jax.experimental import pallas as pl
from jax.experimental.pallas import tpu as pltpu
from jax.sharding import PartitionSpec as P

MOMENT_DECAY = 0.9


def silu_slope(preact):
    sigmoid_value = jax.nn.sigmoid(preact)
    return sigmoid_value * (1.0 + preact * (1.0 - sigmoid_value))


def swap_slots(arrays, partner, slot_count):
    stacked = jnp.stack([array_item.reshape(slot_count, -1) for array_item in arrays], axis=1)
    spread = lax.all_to_all(stacked, "expert", split_axis=0, concat_axis=0, tiled=True)
    picked = jnp.take(spread, partner, axis=0)
    landed = lax.all_to_all(picked, "expert", split_axis=0, concat_axis=0, tiled=True)
    return [landed[:, member].reshape(array_item.shape) for member, array_item in enumerate(arrays)]


def body(
    tokens,
    expert_ids,
    route_weight,
    cotangent,
    holder,
    partner,
    up_weight,
    down_weight,
    up_moment,
    down_moment,
):
    tok_count, top_count = expert_ids.shape
    n_slots = lax.axis_size("expert")
    n_groups = lax.axis_size("dp")
    capacity = min(tok_count, max(2, 4 * tok_count * top_count // (3 * n_slots)))
    feature_count = tokens.shape[1]
    quarter = feature_count // n_groups
    slot_range = jnp.arange(n_slots, dtype=jnp.int32)
    held_hit = (holder[:, None] == slot_range[None, :]).astype(jnp.int32)
    target = jnp.sum(held_hit * partner[None, :], axis=1)
    swapped = swap_slots([up_weight, down_weight, up_moment, down_moment], partner, n_slots)
    up_weight, down_weight, up_moment, down_moment = (
        swapped[0],
        swapped[1],
        swapped[2],
        swapped[3],
    )
    flat_ids = expert_ids.reshape(-1)
    expert_hit = (flat_ids[:, None] == slot_range[None, :]).astype(jnp.int32)
    destination = jnp.sum(expert_hit * target[None, :], axis=1)
    dest_hit = (destination[:, None] == slot_range[None, :]).astype(jnp.int32)
    position = jnp.sum((jnp.cumsum(dest_hit, axis=0) - 1) * dest_hit, axis=1)
    entry_index = destination * capacity + position
    slots_total = n_slots * capacity
    select = (jnp.arange(slots_total, dtype=jnp.int32)[:, None] == entry_index[None, :]).reshape(
        slots_total, tok_count, top_count
    )
    picked = jnp.sum(select.astype(jnp.float32), axis=2)
    scaled = jnp.sum(jnp.where(select, route_weight[None, :, :], 0.0), axis=2)
    sent_rows = jnp.dot(
        picked.astype(jnp.bfloat16), tokens, preferred_element_type=jnp.float32
    ).astype(jnp.bfloat16)
    sent_grads = jnp.dot(
        scaled,
        cotangent.astype(jnp.float32),
        precision=lax.Precision.HIGHEST,
        preferred_element_type=jnp.float32,
    ).astype(jnp.bfloat16)
    outgoing = jnp.stack([sent_rows, sent_grads], axis=0).reshape(
        1, 2, n_slots, capacity, feature_count
    )
    arrived = lax.all_to_all(
        lax.all_to_all(outgoing, "expert", split_axis=2, concat_axis=2, tiled=True),
        "dp",
        split_axis=4,
        concat_axis=0,
        tiled=True,
    )
    rows_in = arrived[:, 0].reshape(-1, quarter)
    grads_in = arrived[:, 1].reshape(-1, quarter)
    up_local = up_weight[0]
    down_local = down_weight[0]
    pre_part = jnp.dot(rows_in, up_local, preferred_element_type=jnp.float32)
    back_part = lax.dot_general(
        grads_in, down_local, (((1,), (1,)), ((), ())), preferred_element_type=jnp.float32
    )
    preact, back_sum = (
        lax.psum(pre_part.astype(jnp.bfloat16), "dp").astype(jnp.float32),
        lax.psum(back_part.astype(jnp.bfloat16), "dp").astype(jnp.float32),
    )
    hidden = jax.nn.silu(preact).astype(jnp.bfloat16)
    pre_grad = (back_sum * silu_slope(preact)).astype(jnp.bfloat16)
    out_part = jnp.dot(hidden, down_local, preferred_element_type=jnp.float32).astype(jnp.bfloat16)
    up_grad = lax.dot_general(
        rows_in, pre_grad, (((0,), (0,)), ((), ())), preferred_element_type=jnp.float32
    )
    down_grad = lax.dot_general(
        hidden, grads_in, (((0,), (0,)), ((), ())), preferred_element_type=jnp.float32
    )
    returned = lax.all_to_all(
        lax.all_to_all(
            out_part.reshape(n_groups, n_slots, capacity, quarter),
            "expert",
            split_axis=1,
            concat_axis=1,
            tiled=True,
        ),
        "dp",
        split_axis=0,
        concat_axis=3,
        tiled=True,
    )
    layer_out = jnp.dot(
        scaled.T,
        returned.reshape(slots_total, feature_count).astype(jnp.float32),
        precision=lax.Precision.HIGHEST,
        preferred_element_type=jnp.float32,
    ).astype(jnp.bfloat16)
    new_up = (
        MOMENT_DECAY * up_moment.astype(jnp.float32) + (1.0 - MOMENT_DECAY) * up_grad[None]
    ).astype(jnp.bfloat16)
    new_down = (
        MOMENT_DECAY * down_moment.astype(jnp.float32) + (1.0 - MOMENT_DECAY) * down_grad[None]
    ).astype(jnp.bfloat16)
    return (layer_out, new_up, new_down)


def own_weights(expert_ids, route_weight, holder, slot_count):
    slot_range = jnp.arange(slot_count, dtype=jnp.int32)
    ids_hit = expert_ids[:, :, None] == slot_range[None, None, :]
    by_expert = jnp.sum(jnp.where(ids_hit, route_weight[:, :, None], 0.0), axis=1)
    placed = holder[:, None] == slot_range[None, :]
    by_slot = jnp.sum(jnp.where(placed[None], by_expert[:, :, None], 0.0), axis=1)
    return by_slot


MESH = pl.DeviceIdType.MESH
CHUNKS = 4


def route_table(partner, me):
    slots = jnp.arange(16, dtype=jnp.int32)
    z, half = me // 4, me // 8
    pair_plane = lax.bitwise_xor(z, 1)
    inner = (z == 1) | (z == 2)
    crosses = (partner // 8) != (slots // 8)
    count = jnp.cumsum(crosses.reshape(2, 8).astype(jnp.int32), axis=1).reshape(16) - 1
    rank = jnp.clip(count, 0, 3)
    quad = jnp.arange(4, dtype=jnp.int32)
    leaving = crosses & (slots // 8 != half)
    hit = leaving[None, :] & (count[None, :] == quad[:, None])
    source = jnp.sum(jnp.where(hit, partner[None, :], 0), axis=1)
    cross_kind = jnp.where(source // 4 == z, 0, 1)
    cross_at = source % 4

    def pick(array_item, start):
        return lax.dynamic_slice(array_item, (start,), (4,))

    pass_source, pass_rank = pick(partner, pair_plane * 4), pick(rank, pair_plane * 4)
    pass_kind = jnp.where(pass_source // 4 == z, 0, 2)
    pass_at = jnp.where(pass_kind == 0, pass_source % 4, pass_rank)
    end_source, end_rank = pick(partner, z * 4), pick(rank, z * 4)
    end_plane = end_source // 4
    inner_kind = jnp.where(end_plane == z, 0, jnp.where(end_plane == pair_plane, 1, 2))
    inner_at = jnp.where(inner_kind == 2, end_rank, end_source % 4)
    outer_kind = jnp.where(end_plane == z, 0, 1)
    outer_at = jnp.where(outer_kind == 0, end_source % 4, quad)
    end_kind = jnp.where(inner, inner_kind, outer_kind)
    end_at = jnp.where(inner, inner_at, outer_at)
    return jnp.concatenate([cross_kind, cross_at, pass_kind, pass_at, end_kind, end_at]).astype(
        jnp.int32
    )


def swap_kernel(*refs):
    table, new_up, new_down, outs, up_end, down_end, layer = refs[:7]
    scratch = list(refs[7:])
    total = 2 * CHUNKS

    def take(number):
        taken = scratch[:number]
        del scratch[:number]
        return taken

    own, pair, cross, landed, passed, final = [take(total) for _ in range(6)]
    plane_in, plane_sum, line_in, core_sum, core_in = take(5)
    (
        spread_send,
        spread_recv,
        pair_send,
        pair_recv,
        cross_send,
        cross_recv,
        end_send,
        end_recv,
        plane_send,
        plane_recv,
        line_send,
        line_recv,
        core_send,
        core_recv,
    ) = scratch
    me = lax.axis_index("expert")
    core = lax.axis_index("dp")
    z, spot = me // 4, me % 4
    inner = (z == 1) | (z == 2)
    plane_peers = [z * 4 + lax.bitwise_xor(spot, r) for r in (1, 2, 3)]
    line_peers = [lax.bitwise_xor(z, r) * 4 + spot for r in (1, 2, 3)]
    pair_peer, cross_peer = line_peers[0], line_peers[2]

    barrier = pltpu.get_barrier_semaphore()
    for peer in plane_peers + line_peers:
        pl.semaphore_signal(barrier, inc=1, device_id=(peer, core), device_id_type=MESH)
    pl.semaphore_signal(barrier, inc=1, device_id=(me, 1 - core), device_id_type=MESH)
    pl.semaphore_wait(barrier, 7)

    sources = [new_up] * CHUNKS + [new_down] * CHUNKS
    ends = [up_end] * CHUNKS + [down_end] * CHUNKS

    def remote(src, dst, send, recv, peer, at_core=None):
        return pltpu.make_async_remote_copy(
            src_ref=src,
            dst_ref=dst,
            send_sem=send,
            recv_sem=recv,
            device_id=(peer, core if at_core is None else at_core),
            device_id_type=MESH,
        )

    def spread(k, r):
        return remote(
            sources[k].at[lax.bitwise_xor(spot, r), k % CHUNKS],
            own[k].at[spot],
            spread_send.at[k, r - 1],
            spread_recv.at[k, r - 1],
            plane_peers[r - 1],
        )

    def finish(k, r):
        return remote(
            final[k].at[lax.bitwise_xor(spot, r)],
            ends[k].at[spot, k % CHUNKS],
            end_send.at[k, r - 1],
            end_recv.at[k, r - 1],
            plane_peers[r - 1],
        )

    def to_pair(k, buffer):
        return remote(buffer, pair[k], pair_send.at[k], pair_recv.at[k], pair_peer)

    def to_cross(k):
        return remote(cross[k], landed[k], cross_send.at[k], cross_recv.at[k], cross_peer)

    def plane_copy(r):
        return remote(
            outs.at[lax.bitwise_xor(spot, r)],
            plane_in.at[r - 1],
            plane_send.at[r - 1],
            plane_recv.at[r - 1],
            plane_peers[r - 1],
        )

    def line_copy(r):
        return remote(
            plane_sum.at[lax.bitwise_xor(z, r)],
            line_in.at[r - 1],
            line_send.at[r - 1],
            line_recv.at[r - 1],
            line_peers[r - 1],
        )

    def core_copy():
        return remote(
            core_sum.at[1 - core], core_in, core_send.at[0], core_recv.at[0], me, 1 - core
        )

    def fill(target, row, pools):
        @pl.loop(0, 4)
        def _(q):
            kind, at = table[row * 8 + q], table[row * 8 + 4 + q]
            value = pools[0][1][at].astype(jnp.float32)
            for code, pool in pools[1:]:
                value = jnp.where(kind == code, pool[at].astype(jnp.float32), value)
            target[q] = value.astype(target.dtype)

    def begin(k):
        for r in (1, 2, 3):
            spread(k, r).start()
        own[k][spot] = sources[k][spot, k % CHUNKS]

    def stage_first(k):
        for r in (1, 2, 3):
            spread(k, r).wait_recv()

        @pl.when(jnp.logical_not(inner))
        def _():
            to_pair(k, own[k]).start()

    def stage_cross(k):
        @pl.when(inner)
        def _():
            to_pair(k, own[k]).wait_recv()
            fill(cross[k], 0, [(0, own[k]), (1, pair[k])])
            to_cross(k).start()

    def stage_pass(k):
        @pl.when(inner)
        def _():
            to_cross(k).wait_recv()
            fill(passed[k], 1, [(0, own[k]), (2, landed[k])])
            to_pair(k, passed[k]).start()
            fill(final[k], 2, [(0, own[k]), (1, pair[k]), (2, landed[k])])
            send_final(k)

    def stage_outer(k):
        @pl.when(jnp.logical_not(inner))
        def _():
            to_pair(k, passed[k]).wait_recv()
            fill(final[k], 2, [(0, own[k]), (1, pair[k])])
            send_final(k)

    def send_final(k):
        for r in (1, 2, 3):
            finish(k, r).start()
        ends[k][spot, k % CHUNKS] = final[k][spot]

    for k in range(CHUNKS):
        begin(k)
    for r in (1, 2, 3):
        plane_copy(r).start()
    for k in range(CHUNKS, total):
        begin(k)

    for step in range(total + 3):
        if step < total:
            stage_first(step)
        if 0 <= step - 1 < total:
            stage_cross(step - 1)
        if 0 <= step - 2 < total:
            stage_pass(step - 2)
        if 0 <= step - 3 < total:
            stage_outer(step - 3)
        if step == CHUNKS:
            for r in (1, 2, 3):
                plane_copy(r).wait_recv()

            @pl.loop(0, 8)
            def _(n):
                at, group = n // 2, n % 2
                value = outs[spot, at, group].astype(jnp.float32)
                for r in range(3):
                    value = value + plane_in[r, at, group].astype(jnp.float32)
                plane_sum[at, group] = value.astype(plane_sum.dtype)

            for r in (1, 2, 3):
                line_copy(r).start()
        if step == CHUNKS + 3:
            for r in (1, 2, 3):
                line_copy(r).wait_recv()
            for group in range(2):
                value = plane_sum[z, group].astype(jnp.float32)
                for r in range(3):
                    value = value + line_in[r, group].astype(jnp.float32)
                core_sum[group] = value.astype(core_sum.dtype)
            core_copy().start()

    core_copy().wait_recv()
    half = core_in.shape[1]
    for group in range(2):

        @pl.when(core == group)
        def _():
            layer[:, group * half : (group + 1) * half] = core_sum[group]
            layer[:, (1 - group) * half : (2 - group) * half] = core_in[...]

    for k in range(total):
        for r in (1, 2, 3):
            finish(k, r).wait_recv()
            finish(k, r).wait_send()
            spread(k, r).wait_send()
        to_pair(k, own[k]).wait_send()

        @pl.when(inner)
        def _():
            to_cross(k).wait_send()

    for r in (1, 2, 3):
        plane_copy(r).wait_send()
        line_copy(r).wait_send()
    core_copy().wait_send()


def swap_and_return(new_up, new_down, outs, partner, me):
    half, hidden_count = new_up.shape
    tok_count = outs.shape[0] // 32
    up_rows, down_rows = half // (4 * CHUNKS), hidden_count // (4 * CHUNKS)
    up_shape = (4, CHUNKS, up_rows, hidden_count)
    down_shape = (4, CHUNKS, down_rows, half)
    kind = new_up.dtype
    pieces = [pltpu.VMEM((4,) + up_shape[2:], kind)] * CHUNKS + [
        pltpu.VMEM((4,) + down_shape[2:], kind)
    ] * CHUNKS
    total = 2 * CHUNKS
    dma = pltpu.SemaphoreType.DMA
    block = (tok_count, half)
    by_spot = outs.reshape(4, 4, 2, tok_count, half).transpose(1, 0, 2, 3, 4)
    vmem = pl.BlockSpec(memory_space=pltpu.VMEM)
    up_end, down_end, layer = pl.pallas_call(
        swap_kernel,
        out_shape=(
            jax.ShapeDtypeStruct(up_shape, kind),
            jax.ShapeDtypeStruct(down_shape, kind),
            jax.ShapeDtypeStruct((tok_count, 2 * half), kind),
        ),
        in_specs=[pl.BlockSpec(memory_space=pltpu.SMEM), vmem, vmem, vmem],
        out_specs=(vmem, vmem, vmem),
        scratch_shapes=pieces * 6
        + [
            pltpu.VMEM((3, 4, 2) + block, kind),
            pltpu.VMEM((4, 2) + block, kind),
            pltpu.VMEM((3, 2) + block, kind),
            pltpu.VMEM((2,) + block, kind),
            pltpu.VMEM(block, kind),
            dma((total, 3)),
            dma((total, 3)),
            dma((total,)),
            dma((total,)),
            dma((total,)),
            dma((total,)),
            dma((total, 3)),
            dma((total, 3)),
            dma((3,)),
            dma((3,)),
            dma((3,)),
            dma((3,)),
            dma((1,)),
            dma((1,)),
        ],
        compiler_params=pltpu.CompilerParams(
            collective_id=1, has_side_effects=True, vmem_limit_bytes=56 * 1024 * 1024
        ),
    )(
        route_table(partner, me),
        new_up.reshape(up_shape),
        new_down.reshape(down_shape),
        by_spot,
    )
    return (
        layer,
        up_end.reshape(1, half, hidden_count),
        down_end.reshape(1, hidden_count, half),
    )


def dense_body(
    tokens,
    expert_ids,
    route_weight,
    cotangent,
    holder,
    partner,
    up_weight,
    down_weight,
    up_moment,
    down_moment,
):
    n_slots = lax.axis_size("expert")
    tok_count, feature_count = tokens.shape
    half = feature_count // 2
    swap_pair = [(0, 1), (1, 0)]
    me = lax.axis_index("expert")
    by_slot = own_weights(expert_ids, route_weight, holder, n_slots)
    gathered_weights = lax.all_gather(by_slot, ("expert", "dp"), axis=0, tiled=True)
    scale = jnp.sum(
        jnp.where(jnp.arange(n_slots)[None, :] == me, gathered_weights, 0.0), axis=1, keepdims=True
    )
    both = lax.all_to_all(
        jnp.stack([tokens, cotangent]), "dp", split_axis=2, concat_axis=1, tiled=True
    )
    every = lax.all_gather(both, "expert", axis=1, tiled=True)
    rows, cots = every[0], every[1]
    grads = (scale * cots.astype(jnp.float32)).astype(jnp.bfloat16)
    up_local, down_local = up_weight[0], down_weight[0]
    pre_part = jnp.dot(rows, up_local, preferred_element_type=jnp.float32).astype(jnp.bfloat16)
    back_part = lax.dot_general(
        grads, down_local, (((1,), (1,)), ((), ())), preferred_element_type=jnp.float32
    ).astype(jnp.bfloat16)
    preact = pre_part.astype(jnp.float32) + lax.ppermute(pre_part, "dp", swap_pair).astype(
        jnp.float32
    )
    back_sum = back_part.astype(jnp.float32) + lax.ppermute(back_part, "dp", swap_pair).astype(
        jnp.float32
    )
    hidden = jax.nn.silu(preact).astype(jnp.bfloat16)
    pre_grad = (back_sum * silu_slope(preact)).astype(jnp.bfloat16)
    up_grad = lax.dot_general(
        rows, pre_grad, (((0,), (0,)), ((), ())), preferred_element_type=jnp.float32
    )
    new_up = (
        MOMENT_DECAY * up_moment[0].astype(jnp.float32) + (1.0 - MOMENT_DECAY) * up_grad
    ).astype(jnp.bfloat16)
    down_grad = lax.dot_general(
        hidden, grads, (((0,), (0,)), ((), ())), preferred_element_type=jnp.float32
    )
    new_down = (
        MOMENT_DECAY * down_moment[0].astype(jnp.float32) + (1.0 - MOMENT_DECAY) * down_grad
    ).astype(jnp.bfloat16)
    out_part = jnp.dot(hidden, down_local, preferred_element_type=jnp.float32).astype(jnp.bfloat16)
    out_part = (scale * out_part.astype(jnp.float32)).astype(jnp.bfloat16)
    return swap_and_return(new_up, new_down, out_part, partner, me)


def pick_body(mesh):
    def chosen(tokens, *others):
        dense = mesh.shape["dp"] == 2 and mesh.shape["expert"] == 16
        return (dense_body if dense else body)(tokens, *others)

    return chosen


def solution(mesh):
    return jax.shard_map(
        pick_body(mesh),
        mesh=mesh,
        in_specs=(
            P(("expert", "dp"), None),
            P(("expert", "dp"), None),
            P(("expert", "dp"), None),
            P(("expert", "dp"), None),
            P(),
            P(),
            P("expert", "dp", None),
            P("expert", None, "dp"),
            P("expert", "dp", None),
            P("expert", None, "dp"),
        ),
        out_specs=(P(("expert", "dp"), None), P("expert", "dp", None), P("expert", None, "dp")),
        check_vma=False,
    )
```

```python
import jax
import jax.numpy as jnp
from jax import lax
from jax.experimental import pallas as pl
from jax.experimental.pallas import tpu as pltpu
from jax.sharding import PartitionSpec as P

MOMENT_DECAY = 0.9


def silu_slope(preact):
    sigmoid_value = jax.nn.sigmoid(preact)
    return sigmoid_value * (1.0 + preact * (1.0 - sigmoid_value))


def swap_slots(arrays, partner, slot_count):
    stacked = jnp.stack([array_item.reshape(slot_count, -1) for array_item in arrays], axis=1)
    spread = lax.all_to_all(stacked, "expert", split_axis=0, concat_axis=0, tiled=True)
    picked = jnp.take(spread, partner, axis=0)
    landed = lax.all_to_all(picked, "expert", split_axis=0, concat_axis=0, tiled=True)
    return [landed[:, member].reshape(array_item.shape) for member, array_item in enumerate(arrays)]


def body(
    tokens,
    expert_ids,
    route_weight,
    cotangent,
    holder,
    partner,
    up_weight,
    down_weight,
    up_moment,
    down_moment,
):
    tok_count, top_count = expert_ids.shape
    n_slots = lax.axis_size("expert")
    n_groups = lax.axis_size("dp")
    capacity = min(tok_count, max(2, 4 * tok_count * top_count // (3 * n_slots)))
    feature_count = tokens.shape[1]
    quarter = feature_count // n_groups
    slot_range = jnp.arange(n_slots, dtype=jnp.int32)
    held_hit = (holder[:, None] == slot_range[None, :]).astype(jnp.int32)
    target = jnp.sum(held_hit * partner[None, :], axis=1)
    swapped = swap_slots([up_weight, down_weight, up_moment, down_moment], partner, n_slots)
    up_weight, down_weight, up_moment, down_moment = (
        swapped[0],
        swapped[1],
        swapped[2],
        swapped[3],
    )
    flat_ids = expert_ids.reshape(-1)
    expert_hit = (flat_ids[:, None] == slot_range[None, :]).astype(jnp.int32)
    destination = jnp.sum(expert_hit * target[None, :], axis=1)
    dest_hit = (destination[:, None] == slot_range[None, :]).astype(jnp.int32)
    position = jnp.sum((jnp.cumsum(dest_hit, axis=0) - 1) * dest_hit, axis=1)
    entry_index = destination * capacity + position
    slots_total = n_slots * capacity
    select = (jnp.arange(slots_total, dtype=jnp.int32)[:, None] == entry_index[None, :]).reshape(
        slots_total, tok_count, top_count
    )
    picked = jnp.sum(select.astype(jnp.float32), axis=2)
    scaled = jnp.sum(jnp.where(select, route_weight[None, :, :], 0.0), axis=2)
    sent_rows = jnp.dot(
        picked.astype(jnp.bfloat16), tokens, preferred_element_type=jnp.float32
    ).astype(jnp.bfloat16)
    sent_grads = jnp.dot(
        scaled,
        cotangent.astype(jnp.float32),
        precision=lax.Precision.HIGHEST,
        preferred_element_type=jnp.float32,
    ).astype(jnp.bfloat16)
    outgoing = jnp.stack([sent_rows, sent_grads], axis=0).reshape(
        1, 2, n_slots, capacity, feature_count
    )
    arrived = lax.all_to_all(
        lax.all_to_all(outgoing, "expert", split_axis=2, concat_axis=2, tiled=True),
        "dp",
        split_axis=4,
        concat_axis=0,
        tiled=True,
    )
    rows_in = arrived[:, 0].reshape(-1, quarter)
    grads_in = arrived[:, 1].reshape(-1, quarter)
    up_local = up_weight[0]
    down_local = down_weight[0]
    pre_part = jnp.dot(rows_in, up_local, preferred_element_type=jnp.float32)
    back_part = lax.dot_general(
        grads_in, down_local, (((1,), (1,)), ((), ())), preferred_element_type=jnp.float32
    )
    preact, back_sum = (
        lax.psum(pre_part.astype(jnp.bfloat16), "dp").astype(jnp.float32),
        lax.psum(back_part.astype(jnp.bfloat16), "dp").astype(jnp.float32),
    )
    hidden = jax.nn.silu(preact).astype(jnp.bfloat16)
    pre_grad = (back_sum * silu_slope(preact)).astype(jnp.bfloat16)
    out_part = jnp.dot(hidden, down_local, preferred_element_type=jnp.float32).astype(jnp.bfloat16)
    up_grad = lax.dot_general(
        rows_in, pre_grad, (((0,), (0,)), ((), ())), preferred_element_type=jnp.float32
    )
    down_grad = lax.dot_general(
        hidden, grads_in, (((0,), (0,)), ((), ())), preferred_element_type=jnp.float32
    )
    returned = lax.all_to_all(
        lax.all_to_all(
            out_part.reshape(n_groups, n_slots, capacity, quarter),
            "expert",
            split_axis=1,
            concat_axis=1,
            tiled=True,
        ),
        "dp",
        split_axis=0,
        concat_axis=3,
        tiled=True,
    )
    layer_out = jnp.dot(
        scaled.T,
        returned.reshape(slots_total, feature_count).astype(jnp.float32),
        precision=lax.Precision.HIGHEST,
        preferred_element_type=jnp.float32,
    ).astype(jnp.bfloat16)
    new_up = (
        MOMENT_DECAY * up_moment.astype(jnp.float32) + (1.0 - MOMENT_DECAY) * up_grad[None]
    ).astype(jnp.bfloat16)
    new_down = (
        MOMENT_DECAY * down_moment.astype(jnp.float32) + (1.0 - MOMENT_DECAY) * down_grad[None]
    ).astype(jnp.bfloat16)
    return (layer_out, new_up, new_down)


def own_weights(expert_ids, route_weight, holder, slot_count):
    slot_range = jnp.arange(slot_count, dtype=jnp.int32)
    ids_hit = expert_ids[:, :, None] == slot_range[None, None, :]
    by_expert = jnp.sum(jnp.where(ids_hit, route_weight[:, :, None], 0.0), axis=1)
    placed = holder[:, None] == slot_range[None, :]
    by_slot = jnp.sum(jnp.where(placed[None], by_expert[:, :, None], 0.0), axis=1)
    return by_slot


MESH = pl.DeviceIdType.MESH
CHUNKS = 4


def route_table(partner, me):
    slots = jnp.arange(16, dtype=jnp.int32)
    z, half = me // 4, me // 8
    pair_plane = lax.bitwise_xor(z, 1)
    inner = (z == 1) | (z == 2)
    crosses = (partner // 8) != (slots // 8)
    count = jnp.cumsum(crosses.reshape(2, 8).astype(jnp.int32), axis=1).reshape(16) - 1
    rank = jnp.clip(count, 0, 3)
    quad = jnp.arange(4, dtype=jnp.int32)
    leaving = crosses & (slots // 8 != half)
    hit = leaving[None, :] & (count[None, :] == quad[:, None])
    source = jnp.sum(jnp.where(hit, partner[None, :], 0), axis=1)
    cross_kind = jnp.where(source // 4 == z, 0, 1)
    cross_at = source % 4

    def pick(array_item, start):
        return lax.dynamic_slice(array_item, (start,), (4,))

    pass_source, pass_rank = pick(partner, pair_plane * 4), pick(rank, pair_plane * 4)
    pass_kind = jnp.where(pass_source // 4 == z, 0, 2)
    pass_at = jnp.where(pass_kind == 0, pass_source % 4, pass_rank)
    end_source, end_rank = pick(partner, z * 4), pick(rank, z * 4)
    end_plane = end_source // 4
    inner_kind = jnp.where(end_plane == z, 0, jnp.where(end_plane == pair_plane, 1, 2))
    inner_at = jnp.where(inner_kind == 2, end_rank, end_source % 4)
    outer_kind = jnp.where(end_plane == z, 0, 1)
    outer_at = jnp.where(outer_kind == 0, end_source % 4, quad)
    end_kind = jnp.where(inner, inner_kind, outer_kind)
    end_at = jnp.where(inner, inner_at, outer_at)
    return jnp.concatenate([cross_kind, cross_at, pass_kind, pass_at, end_kind, end_at]).astype(
        jnp.int32
    )


def swap_kernel(*refs):
    table, new_up, new_down, outs, up_end, down_end, layer = refs[:7]
    scratch = list(refs[7:])
    total = 2 * CHUNKS

    def take(number):
        taken = scratch[:number]
        del scratch[:number]
        return taken

    own, pair, cross, landed, passed, final = [take(total) for _ in range(6)]
    plane_in, plane_sum, line_in, core_sum, core_in = take(5)
    (
        spread_send,
        spread_recv,
        pair_send,
        pair_recv,
        cross_send,
        cross_recv,
        end_send,
        end_recv,
        plane_send,
        plane_recv,
        line_send,
        line_recv,
        core_send,
        core_recv,
    ) = scratch
    me = lax.axis_index("expert")
    core = lax.axis_index("dp")
    z, spot = me // 4, me % 4
    inner = (z == 1) | (z == 2)
    plane_peers = [z * 4 + lax.bitwise_xor(spot, r) for r in (1, 2, 3)]
    line_peers = [lax.bitwise_xor(z, r) * 4 + spot for r in (1, 2, 3)]
    pair_peer, cross_peer = line_peers[0], line_peers[2]

    barrier = pltpu.get_barrier_semaphore()
    for peer in plane_peers + line_peers:
        pl.semaphore_signal(barrier, inc=1, device_id=(peer, core), device_id_type=MESH)
    pl.semaphore_signal(barrier, inc=1, device_id=(me, 1 - core), device_id_type=MESH)
    pl.semaphore_wait(barrier, 7)

    sources = [new_up] * CHUNKS + [new_down] * CHUNKS
    ends = [up_end] * CHUNKS + [down_end] * CHUNKS

    def remote(src, dst, send, recv, peer, at_core=None):
        return pltpu.make_async_remote_copy(
            src_ref=src,
            dst_ref=dst,
            send_sem=send,
            recv_sem=recv,
            device_id=(peer, core if at_core is None else at_core),
            device_id_type=MESH,
        )

    def spread(k, r):
        return remote(
            sources[k].at[lax.bitwise_xor(spot, r), k % CHUNKS],
            own[k].at[spot],
            spread_send.at[k, r - 1],
            spread_recv.at[k, r - 1],
            plane_peers[r - 1],
        )

    def finish(k, r):
        return remote(
            final[k].at[lax.bitwise_xor(spot, r)],
            ends[k].at[spot, k % CHUNKS],
            end_send.at[k, r - 1],
            end_recv.at[k, r - 1],
            plane_peers[r - 1],
        )

    def to_pair(k, buffer):
        return remote(buffer, pair[k], pair_send.at[k], pair_recv.at[k], pair_peer)

    def to_cross(k):
        return remote(cross[k], landed[k], cross_send.at[k], cross_recv.at[k], cross_peer)

    def plane_copy(r):
        return remote(
            outs.at[lax.bitwise_xor(spot, r)],
            plane_in.at[r - 1],
            plane_send.at[r - 1],
            plane_recv.at[r - 1],
            plane_peers[r - 1],
        )

    def line_copy(r):
        return remote(
            plane_sum.at[lax.bitwise_xor(z, r)],
            line_in.at[r - 1],
            line_send.at[r - 1],
            line_recv.at[r - 1],
            line_peers[r - 1],
        )

    def core_copy():
        return remote(
            core_sum.at[1 - core], core_in, core_send.at[0], core_recv.at[0], me, 1 - core
        )

    def fill(target, row, pools):
        @pl.loop(0, 4)
        def _(q):
            kind, at = table[row * 8 + q], table[row * 8 + 4 + q]
            value = pools[0][1][at].astype(jnp.float32)
            for code, pool in pools[1:]:
                value = jnp.where(kind == code, pool[at].astype(jnp.float32), value)
            target[q] = value.astype(target.dtype)

    def begin(k):
        for r in (1, 2, 3):
            spread(k, r).start()
        own[k][spot] = sources[k][spot, k % CHUNKS]

    def stage_first(k):
        for r in (1, 2, 3):
            spread(k, r).wait_recv()

        @pl.when(jnp.logical_not(inner))
        def _():
            to_pair(k, own[k]).start()

    def stage_cross(k):
        @pl.when(inner)
        def _():
            to_pair(k, own[k]).wait_recv()
            fill(cross[k], 0, [(0, own[k]), (1, pair[k])])
            to_cross(k).start()

    def stage_pass(k):
        @pl.when(inner)
        def _():
            to_cross(k).wait_recv()
            fill(passed[k], 1, [(0, own[k]), (2, landed[k])])
            to_pair(k, passed[k]).start()
            fill(final[k], 2, [(0, own[k]), (1, pair[k]), (2, landed[k])])
            send_final(k)

    def stage_outer(k):
        @pl.when(jnp.logical_not(inner))
        def _():
            to_pair(k, passed[k]).wait_recv()
            fill(final[k], 2, [(0, own[k]), (1, pair[k])])
            send_final(k)

    def send_final(k):
        for r in (1, 2, 3):
            finish(k, r).start()
        ends[k][spot, k % CHUNKS] = final[k][spot]

    for k in range(CHUNKS):
        begin(k)
    for r in (1, 2, 3):
        plane_copy(r).start()
    for k in range(CHUNKS, total):
        begin(k)

    for step in range(total + 3):
        if step < total:
            stage_first(step)
        if 0 <= step - 1 < total:
            stage_cross(step - 1)
        if 0 <= step - 2 < total:
            stage_pass(step - 2)
        if 0 <= step - 3 < total:
            stage_outer(step - 3)
        if step == CHUNKS:
            for r in (1, 2, 3):
                plane_copy(r).wait_recv()

            @pl.loop(0, 8)
            def _(n):
                at, group = n // 2, n % 2
                value = outs[spot, at, group].astype(jnp.float32)
                for r in range(3):
                    value = value + plane_in[r, at, group].astype(jnp.float32)
                plane_sum[at, group] = value.astype(plane_sum.dtype)

            for r in (1, 2, 3):
                line_copy(r).start()
        if step == CHUNKS + 3:
            for r in (1, 2, 3):
                line_copy(r).wait_recv()
            for group in range(2):
                value = plane_sum[z, group].astype(jnp.float32)
                for r in range(3):
                    value = value + line_in[r, group].astype(jnp.float32)
                core_sum[group] = value.astype(core_sum.dtype)
            core_copy().start()

    core_copy().wait_recv()
    half = core_in.shape[1]
    for group in range(2):

        @pl.when(core == group)
        def _():
            layer[:, group * half : (group + 1) * half] = core_sum[group]
            layer[:, (1 - group) * half : (2 - group) * half] = core_in[...]

    for k in range(total):
        for r in (1, 2, 3):
            finish(k, r).wait_recv()
            finish(k, r).wait_send()
            spread(k, r).wait_send()
        to_pair(k, own[k]).wait_send()

        @pl.when(inner)
        def _():
            to_cross(k).wait_send()

    for r in (1, 2, 3):
        plane_copy(r).wait_send()
        line_copy(r).wait_send()
    core_copy().wait_send()


def swap_and_return(new_up, new_down, outs, partner, me):
    half, hidden_count = new_up.shape
    tok_count = outs.shape[0] // 32
    up_rows, down_rows = half // (4 * CHUNKS), hidden_count // (4 * CHUNKS)
    up_shape = (4, CHUNKS, up_rows, hidden_count)
    down_shape = (4, CHUNKS, down_rows, half)
    kind = new_up.dtype
    pieces = [pltpu.VMEM((4,) + up_shape[2:], kind)] * CHUNKS + [
        pltpu.VMEM((4,) + down_shape[2:], kind)
    ] * CHUNKS
    total = 2 * CHUNKS
    dma = pltpu.SemaphoreType.DMA
    block = (tok_count, half)
    by_spot = outs.reshape(4, 4, 2, tok_count, half).transpose(1, 0, 2, 3, 4)
    vmem = pl.BlockSpec(memory_space=pltpu.VMEM)
    up_end, down_end, layer = pl.pallas_call(
        swap_kernel,
        out_shape=(
            jax.ShapeDtypeStruct(up_shape, kind),
            jax.ShapeDtypeStruct(down_shape, kind),
            jax.ShapeDtypeStruct((tok_count, 2 * half), kind),
        ),
        in_specs=[pl.BlockSpec(memory_space=pltpu.SMEM), vmem, vmem, vmem],
        out_specs=(vmem, vmem, vmem),
        scratch_shapes=pieces * 6
        + [
            pltpu.VMEM((3, 4, 2) + block, kind),
            pltpu.VMEM((4, 2) + block, kind),
            pltpu.VMEM((3, 2) + block, kind),
            pltpu.VMEM((2,) + block, kind),
            pltpu.VMEM(block, kind),
            dma((total, 3)),
            dma((total, 3)),
            dma((total,)),
            dma((total,)),
            dma((total,)),
            dma((total,)),
            dma((total, 3)),
            dma((total, 3)),
            dma((3,)),
            dma((3,)),
            dma((3,)),
            dma((3,)),
            dma((1,)),
            dma((1,)),
        ],
        compiler_params=pltpu.CompilerParams(
            collective_id=1, has_side_effects=True, vmem_limit_bytes=56 * 1024 * 1024
        ),
    )(
        route_table(partner, me),
        new_up.reshape(up_shape),
        new_down.reshape(down_shape),
        by_spot,
    )
    return (
        layer,
        up_end.reshape(1, half, hidden_count),
        down_end.reshape(1, hidden_count, half),
    )


def gather_kernel(*refs):
    arrays, ends = refs[:3], refs[3:6]
    line_send, line_recv, near_send, near_recv, far_send, far_recv = refs[6:]
    me = lax.axis_index("expert")
    core = lax.axis_index("dp")
    z, spot = me // 4, me % 4
    near = [z * 4 + lax.bitwise_xor(spot, r) for r in (1, 2)]
    line = [lax.bitwise_xor(z, r) * 4 + spot for r in range(4)]
    hops = [(r, flip) for r in (0, 1, 2, 3) for flip in (0, 1) if r + flip > 0]

    barrier = pltpu.get_barrier_semaphore()
    for r, flip in hops:
        pl.semaphore_signal(
            barrier,
            inc=1,
            device_id=(line[r], lax.bitwise_xor(core, flip)),
            device_id_type=MESH,
        )
    for peer in near:
        pl.semaphore_signal(barrier, inc=1, device_id=(peer, core), device_id_type=MESH)
    pl.semaphore_wait(barrier, len(hops) + 2)

    def line_copy(a, r, flip):
        at_core = lax.bitwise_xor(core, flip)
        return pltpu.make_async_remote_copy(
            src_ref=arrays[a] if a == 2 else arrays[a].at[at_core],
            dst_ref=ends[a].at[me, core],
            send_sem=line_send.at[a, r * 2 + flip],
            recv_sem=line_recv.at[a, r * 2 + flip],
            device_id=(line[r], at_core),
            device_id_type=MESH,
        )

    def near_copy(a, r, way):
        block = ends[a].at[line[r]]
        return pltpu.make_async_remote_copy(
            src_ref=block,
            dst_ref=block,
            send_sem=near_send.at[a, r, way],
            recv_sem=near_recv.at[a, r, way],
            device_id=(near[way], core),
            device_id_type=MESH,
        )

    def far_copy(a, r):
        came = 1 if a == 1 else 0
        block = ends[a].at[lax.bitwise_xor(z, r) * 4 + lax.bitwise_xor(spot, came + 1)]
        return pltpu.make_async_remote_copy(
            src_ref=block,
            dst_ref=block,
            send_sem=far_send.at[a, r],
            recv_sem=far_recv.at[a, r],
            device_id=(near[1 - came], core),
            device_id_type=MESH,
        )

    for r, flip in hops:
        for a in range(3):
            line_copy(a, r, flip).start()
    for a in range(2):
        ends[a][me, core] = arrays[a][core]
    ends[2][me, core] = arrays[2][...]

    for step in range(5):
        if step < 4:
            for a in range(3):
                for flip in (0, 1):
                    if step + flip > 0:
                        line_copy(a, step, flip).wait_recv()
                for way in (0, 1):
                    near_copy(a, step, way).start()
        if step >= 1:
            for a in range(3):
                came = 1 if a == 1 else 0
                near_copy(a, step - 1, came).wait_recv()
                far_copy(a, step - 1).start()

    for a in range(3):
        for r in range(4):
            near_copy(a, r, 0 if a == 1 else 1).wait_recv()
            far_copy(a, r).wait_recv()
            far_copy(a, r).wait_send()
            for way in (0, 1):
                near_copy(a, r, way).wait_send()
        for r, flip in hops:
            line_copy(a, r, flip).wait_send()


def gather_tokens(tokens, cotangent, by_slot, me):
    tok_count, feature_count = tokens.shape
    half = feature_count // 2
    kind = tokens.dtype

    def by_half(array_item):
        return array_item.reshape(tok_count, 2, half).transpose(1, 0, 2)

    flat = by_slot.T.reshape(-1, 128)
    table_rows = flat.shape[0]
    flat = jnp.pad(flat, ((0, 8 - table_rows), (0, 0)))
    vmem = pl.BlockSpec(memory_space=pltpu.VMEM)
    dma = pltpu.SemaphoreType.DMA
    full = jax.ShapeDtypeStruct((16, 2, tok_count, half), kind)
    rows, cots, tables = pl.pallas_call(
        gather_kernel,
        out_shape=(full, full, jax.ShapeDtypeStruct((16, 2, 8, 128), jnp.float32)),
        in_specs=[vmem] * 3,
        out_specs=(vmem,) * 3,
        scratch_shapes=[
            dma((3, 8)),
            dma((3, 8)),
            dma((3, 4, 2)),
            dma((3, 4, 2)),
            dma((3, 4)),
            dma((3, 4)),
        ],
        compiler_params=pltpu.CompilerParams(
            collective_id=2, has_side_effects=True, vmem_limit_bytes=32 * 1024 * 1024
        ),
    )(by_half(tokens), by_half(cotangent), flat)
    weights = tables[:, :, :table_rows].reshape(32, 16, tok_count)
    hit = jnp.arange(16)[None, :, None] == me
    scale = jnp.sum(jnp.where(hit, weights, 0.0), axis=1).reshape(-1, 1)
    return rows.reshape(-1, half), cots.reshape(-1, half), scale


def dense_body(
    tokens,
    expert_ids,
    route_weight,
    cotangent,
    holder,
    partner,
    up_weight,
    down_weight,
    up_moment,
    down_moment,
):
    n_slots = lax.axis_size("expert")
    swap_pair = [(0, 1), (1, 0)]
    me = lax.axis_index("expert")
    by_slot = own_weights(expert_ids, route_weight, holder, n_slots)
    rows, cots, scale = gather_tokens(tokens, cotangent, by_slot, me)
    grads = (scale * cots.astype(jnp.float32)).astype(jnp.bfloat16)
    up_local, down_local = up_weight[0], down_weight[0]
    pre_part = jnp.dot(rows, up_local, preferred_element_type=jnp.float32).astype(jnp.bfloat16)
    back_part = lax.dot_general(
        grads, down_local, (((1,), (1,)), ((), ())), preferred_element_type=jnp.float32
    ).astype(jnp.bfloat16)
    preact = pre_part.astype(jnp.float32) + lax.ppermute(pre_part, "dp", swap_pair).astype(
        jnp.float32
    )
    back_sum = back_part.astype(jnp.float32) + lax.ppermute(back_part, "dp", swap_pair).astype(
        jnp.float32
    )
    hidden = jax.nn.silu(preact).astype(jnp.bfloat16)
    pre_grad = (back_sum * silu_slope(preact)).astype(jnp.bfloat16)
    up_grad = lax.dot_general(
        rows, pre_grad, (((0,), (0,)), ((), ())), preferred_element_type=jnp.float32
    )
    new_up = (
        MOMENT_DECAY * up_moment[0].astype(jnp.float32) + (1.0 - MOMENT_DECAY) * up_grad
    ).astype(jnp.bfloat16)
    down_grad = lax.dot_general(
        hidden, grads, (((0,), (0,)), ((), ())), preferred_element_type=jnp.float32
    )
    new_down = (
        MOMENT_DECAY * down_moment[0].astype(jnp.float32) + (1.0 - MOMENT_DECAY) * down_grad
    ).astype(jnp.bfloat16)
    out_part = jnp.dot(hidden, down_local, preferred_element_type=jnp.float32).astype(jnp.bfloat16)
    out_part = (scale * out_part.astype(jnp.float32)).astype(jnp.bfloat16)
    return swap_and_return(new_up, new_down, out_part, partner, me)


def pick_body(mesh):
    def chosen(tokens, *others):
        dense = mesh.shape["dp"] == 2 and mesh.shape["expert"] == 16
        return (dense_body if dense else body)(tokens, *others)

    return chosen


def solution(mesh):
    return jax.shard_map(
        pick_body(mesh),
        mesh=mesh,
        in_specs=(
            P(("expert", "dp"), None),
            P(("expert", "dp"), None),
            P(("expert", "dp"), None),
            P(("expert", "dp"), None),
            P(),
            P(),
            P("expert", "dp", None),
            P("expert", None, "dp"),
            P("expert", "dp", None),
            P("expert", None, "dp"),
        ),
        out_specs=(P(("expert", "dp"), None), P("expert", "dp", None), P("expert", None, "dp")),
        check_vma=False,
    )
```

```python
import jax
import jax.numpy as jnp
from jax import lax
from jax.experimental import pallas as pl
from jax.experimental.pallas import tpu as pltpu
from jax.sharding import PartitionSpec as P

MOMENT_DECAY = 0.9


def silu_slope(preact):
    sigmoid_value = jax.nn.sigmoid(preact)
    return sigmoid_value * (1.0 + preact * (1.0 - sigmoid_value))


def swap_slots(arrays, partner, slot_count):
    stacked = jnp.stack([array_item.reshape(slot_count, -1) for array_item in arrays], axis=1)
    spread = lax.all_to_all(stacked, "expert", split_axis=0, concat_axis=0, tiled=True)
    picked = jnp.take(spread, partner, axis=0)
    landed = lax.all_to_all(picked, "expert", split_axis=0, concat_axis=0, tiled=True)
    return [landed[:, member].reshape(array_item.shape) for member, array_item in enumerate(arrays)]


def body(
    tokens,
    expert_ids,
    route_weight,
    cotangent,
    holder,
    partner,
    up_weight,
    down_weight,
    up_moment,
    down_moment,
):
    tok_count, top_count = expert_ids.shape
    n_slots = lax.axis_size("expert")
    n_groups = lax.axis_size("dp")
    capacity = min(tok_count, max(2, 4 * tok_count * top_count // (3 * n_slots)))
    feature_count = tokens.shape[1]
    quarter = feature_count // n_groups
    slot_range = jnp.arange(n_slots, dtype=jnp.int32)
    held_hit = (holder[:, None] == slot_range[None, :]).astype(jnp.int32)
    target = jnp.sum(held_hit * partner[None, :], axis=1)
    swapped = swap_slots([up_weight, down_weight, up_moment, down_moment], partner, n_slots)
    up_weight, down_weight, up_moment, down_moment = (
        swapped[0],
        swapped[1],
        swapped[2],
        swapped[3],
    )
    flat_ids = expert_ids.reshape(-1)
    expert_hit = (flat_ids[:, None] == slot_range[None, :]).astype(jnp.int32)
    destination = jnp.sum(expert_hit * target[None, :], axis=1)
    dest_hit = (destination[:, None] == slot_range[None, :]).astype(jnp.int32)
    position = jnp.sum((jnp.cumsum(dest_hit, axis=0) - 1) * dest_hit, axis=1)
    entry_index = destination * capacity + position
    slots_total = n_slots * capacity
    select = (jnp.arange(slots_total, dtype=jnp.int32)[:, None] == entry_index[None, :]).reshape(
        slots_total, tok_count, top_count
    )
    picked = jnp.sum(select.astype(jnp.float32), axis=2)
    scaled = jnp.sum(jnp.where(select, route_weight[None, :, :], 0.0), axis=2)
    sent_rows = jnp.dot(
        picked.astype(jnp.bfloat16), tokens, preferred_element_type=jnp.float32
    ).astype(jnp.bfloat16)
    sent_grads = jnp.dot(
        scaled,
        cotangent.astype(jnp.float32),
        precision=lax.Precision.HIGHEST,
        preferred_element_type=jnp.float32,
    ).astype(jnp.bfloat16)
    outgoing = jnp.stack([sent_rows, sent_grads], axis=0).reshape(
        1, 2, n_slots, capacity, feature_count
    )
    arrived = lax.all_to_all(
        lax.all_to_all(outgoing, "expert", split_axis=2, concat_axis=2, tiled=True),
        "dp",
        split_axis=4,
        concat_axis=0,
        tiled=True,
    )
    rows_in = arrived[:, 0].reshape(-1, quarter)
    grads_in = arrived[:, 1].reshape(-1, quarter)
    up_local = up_weight[0]
    down_local = down_weight[0]
    pre_part = jnp.dot(rows_in, up_local, preferred_element_type=jnp.float32)
    back_part = lax.dot_general(
        grads_in, down_local, (((1,), (1,)), ((), ())), preferred_element_type=jnp.float32
    )
    preact, back_sum = (
        lax.psum(pre_part.astype(jnp.bfloat16), "dp").astype(jnp.float32),
        lax.psum(back_part.astype(jnp.bfloat16), "dp").astype(jnp.float32),
    )
    hidden = jax.nn.silu(preact).astype(jnp.bfloat16)
    pre_grad = (back_sum * silu_slope(preact)).astype(jnp.bfloat16)
    out_part = jnp.dot(hidden, down_local, preferred_element_type=jnp.float32).astype(jnp.bfloat16)
    up_grad = lax.dot_general(
        rows_in, pre_grad, (((0,), (0,)), ((), ())), preferred_element_type=jnp.float32
    )
    down_grad = lax.dot_general(
        hidden, grads_in, (((0,), (0,)), ((), ())), preferred_element_type=jnp.float32
    )
    returned = lax.all_to_all(
        lax.all_to_all(
            out_part.reshape(n_groups, n_slots, capacity, quarter),
            "expert",
            split_axis=1,
            concat_axis=1,
            tiled=True,
        ),
        "dp",
        split_axis=0,
        concat_axis=3,
        tiled=True,
    )
    layer_out = jnp.dot(
        scaled.T,
        returned.reshape(slots_total, feature_count).astype(jnp.float32),
        precision=lax.Precision.HIGHEST,
        preferred_element_type=jnp.float32,
    ).astype(jnp.bfloat16)
    new_up = (
        MOMENT_DECAY * up_moment.astype(jnp.float32) + (1.0 - MOMENT_DECAY) * up_grad[None]
    ).astype(jnp.bfloat16)
    new_down = (
        MOMENT_DECAY * down_moment.astype(jnp.float32) + (1.0 - MOMENT_DECAY) * down_grad[None]
    ).astype(jnp.bfloat16)
    return (layer_out, new_up, new_down)


def own_weights(expert_ids, route_weight, holder, slot_count):
    slot_range = jnp.arange(slot_count, dtype=jnp.int32)
    ids_hit = expert_ids[:, :, None] == slot_range[None, None, :]
    by_expert = jnp.sum(jnp.where(ids_hit, route_weight[:, :, None], 0.0), axis=1)
    placed = holder[:, None] == slot_range[None, :]
    by_slot = jnp.sum(jnp.where(placed[None], by_expert[:, :, None], 0.0), axis=1)
    return by_slot


MESH = pl.DeviceIdType.MESH
UP_CHUNKS = 8
DOWN_CHUNKS = 6
CHUNKS = UP_CHUNKS + DOWN_CHUNKS
AHEAD = 2


def route_table(partner, me):
    slots = jnp.arange(16, dtype=jnp.int32)
    z, half = me // 4, me // 8
    pair_plane = lax.bitwise_xor(z, 1)
    inner = (z == 1) | (z == 2)
    crosses = (partner // 8) != (slots // 8)
    count = jnp.cumsum(crosses.reshape(2, 8).astype(jnp.int32), axis=1).reshape(16) - 1
    rank = jnp.clip(count, 0, 3)
    quad = jnp.arange(4, dtype=jnp.int32)
    leaving = crosses & (slots // 8 != half)
    hit = leaving[None, :] & (count[None, :] == quad[:, None])
    source = jnp.sum(jnp.where(hit, partner[None, :], 0), axis=1)
    cross_kind = jnp.where(source // 4 == z, 0, 1)
    cross_at = source % 4

    def pick(array_item, start):
        return lax.dynamic_slice(array_item, (start,), (4,))

    pass_source, pass_rank = pick(partner, pair_plane * 4), pick(rank, pair_plane * 4)
    pass_kind = jnp.where(pass_source // 4 == z, 0, 2)
    pass_at = jnp.where(pass_kind == 0, pass_source % 4, pass_rank)
    end_source, end_rank = pick(partner, z * 4), pick(rank, z * 4)
    end_plane = end_source // 4
    inner_kind = jnp.where(end_plane == z, 0, jnp.where(end_plane == pair_plane, 1, 2))
    inner_at = jnp.where(inner_kind == 2, end_rank, end_source % 4)
    outer_kind = jnp.where(end_plane == z, 0, 1)
    outer_at = jnp.where(outer_kind == 0, end_source % 4, quad)
    end_kind = jnp.where(inner, inner_kind, outer_kind)
    end_at = jnp.where(inner, inner_at, outer_at)
    return jnp.concatenate([cross_kind, cross_at, pass_kind, pass_at, end_kind, end_at]).astype(
        jnp.int32
    )


def swap_kernel(*refs):
    table, new_up, new_down, outs, up_end, down_end, layer = refs[:7]
    scratch = list(refs[7:])
    total = CHUNKS

    def take(number):
        taken = scratch[:number]
        del scratch[:number]
        return taken

    own, pair, cross, landed, passed, final = [take(total) for _ in range(6)]
    plane_in, plane_sum, line_in, core_sum, core_in = take(5)
    (
        spread_send,
        spread_recv,
        pair_send,
        pair_recv,
        cross_send,
        cross_recv,
        end_send,
        end_recv,
        plane_send,
        plane_recv,
        line_send,
        line_recv,
        core_send,
        core_recv,
    ) = scratch
    me = lax.axis_index("expert")
    core = lax.axis_index("dp")
    z, spot = me // 4, me % 4
    inner = (z == 1) | (z == 2)
    plane_peers = [z * 4 + lax.bitwise_xor(spot, r) for r in (1, 2, 3)]
    line_peers = [lax.bitwise_xor(z, r) * 4 + spot for r in (1, 2, 3)]
    pair_peer, cross_peer = line_peers[0], line_peers[2]

    barrier = pltpu.get_barrier_semaphore()
    for peer in plane_peers + line_peers:
        pl.semaphore_signal(barrier, inc=1, device_id=(peer, core), device_id_type=MESH)
    pl.semaphore_signal(barrier, inc=1, device_id=(me, 1 - core), device_id_type=MESH)
    pl.semaphore_wait(barrier, 7)

    sources = [new_up] * UP_CHUNKS + [new_down] * DOWN_CHUNKS
    ends = [up_end] * UP_CHUNKS + [down_end] * DOWN_CHUNKS
    places = list(range(UP_CHUNKS)) + list(range(DOWN_CHUNKS))

    def remote(src, dst, send, recv, peer, at_core=None):
        return pltpu.make_async_remote_copy(
            src_ref=src,
            dst_ref=dst,
            send_sem=send,
            recv_sem=recv,
            device_id=(peer, core if at_core is None else at_core),
            device_id_type=MESH,
        )

    def spread(k, r):
        return remote(
            sources[k].at[lax.bitwise_xor(spot, r), places[k]],
            own[k].at[spot],
            spread_send.at[k, r - 1],
            spread_recv.at[k, r - 1],
            plane_peers[r - 1],
        )

    def finish(k, r):
        return remote(
            final[k].at[lax.bitwise_xor(spot, r)],
            ends[k].at[spot, places[k]],
            end_send.at[k, r - 1],
            end_recv.at[k, r - 1],
            plane_peers[r - 1],
        )

    def to_pair(k, buffer):
        return remote(buffer, pair[k], pair_send.at[k], pair_recv.at[k], pair_peer)

    def to_cross(k):
        return remote(cross[k], landed[k], cross_send.at[k], cross_recv.at[k], cross_peer)

    def plane_copy(r):
        return remote(
            outs.at[lax.bitwise_xor(spot, r)],
            plane_in.at[r - 1],
            plane_send.at[r - 1],
            plane_recv.at[r - 1],
            plane_peers[r - 1],
        )

    def line_copy(r):
        return remote(
            plane_sum.at[lax.bitwise_xor(z, r)],
            line_in.at[r - 1],
            line_send.at[r - 1],
            line_recv.at[r - 1],
            line_peers[r - 1],
        )

    def core_copy():
        return remote(
            core_sum.at[1 - core], core_in, core_send.at[0], core_recv.at[0], me, 1 - core
        )

    def fill(target, row, pools):
        @pl.loop(0, 4)
        def _(q):
            kind, at = table[row * 8 + q], table[row * 8 + 4 + q]
            value = pools[0][1][at].astype(jnp.float32)
            for code, pool in pools[1:]:
                value = jnp.where(kind == code, pool[at].astype(jnp.float32), value)
            target[q] = value.astype(target.dtype)

    def begin(k):
        for r in (1, 2, 3):
            spread(k, r).start()
        own[k][spot] = sources[k][spot, places[k]]

    def stage_first(k):
        for r in (1, 2, 3):
            spread(k, r).wait_recv()

        @pl.when(jnp.logical_not(inner))
        def _():
            to_pair(k, own[k]).start()

    def stage_cross(k):
        @pl.when(inner)
        def _():
            to_pair(k, own[k]).wait_recv()
            fill(cross[k], 0, [(0, own[k]), (1, pair[k])])
            to_cross(k).start()

    def stage_pass(k):
        @pl.when(inner)
        def _():
            to_cross(k).wait_recv()
            fill(passed[k], 1, [(0, own[k]), (2, landed[k])])
            to_pair(k, passed[k]).start()
            fill(final[k], 2, [(0, own[k]), (1, pair[k]), (2, landed[k])])
            send_final(k)

    def stage_outer(k):
        @pl.when(jnp.logical_not(inner))
        def _():
            to_pair(k, passed[k]).wait_recv()
            fill(final[k], 2, [(0, own[k]), (1, pair[k])])
            send_final(k)

    def send_final(k):
        for r in (1, 2, 3):
            finish(k, r).start()
        ends[k][spot, places[k]] = final[k][spot]

    for k in range(AHEAD):
        begin(k)

    for step in range(total + 3):
        if step < total:
            stage_first(step)
        if step + AHEAD < total:
            begin(step + AHEAD)
        if step == 0:
            for r in (1, 2, 3):
                plane_copy(r).start()
        if 0 <= step - 1 < total:
            stage_cross(step - 1)
        if 0 <= step - 2 < total:
            stage_pass(step - 2)
        if 0 <= step - 3 < total:
            stage_outer(step - 3)
        if step == 7:
            for r in (1, 2, 3):
                plane_copy(r).wait_recv()

            @pl.loop(0, 8)
            def _(n):
                at, group = n // 2, n % 2
                value = outs[spot, at, group].astype(jnp.float32)
                for r in range(3):
                    value = value + plane_in[r, at, group].astype(jnp.float32)
                plane_sum[at, group] = value.astype(plane_sum.dtype)

            for r in (1, 2, 3):
                line_copy(r).start()
        if step == 11:
            for r in (1, 2, 3):
                line_copy(r).wait_recv()
            for group in range(2):
                value = plane_sum[z, group].astype(jnp.float32)
                for r in range(3):
                    value = value + line_in[r, group].astype(jnp.float32)
                core_sum[group] = value.astype(core_sum.dtype)
            core_copy().start()

    core_copy().wait_recv()
    half = core_in.shape[1]
    for group in range(2):

        @pl.when(core == group)
        def _():
            layer[:, group * half : (group + 1) * half] = core_sum[group]
            layer[:, (1 - group) * half : (2 - group) * half] = core_in[...]

    for k in range(total):
        for r in (1, 2, 3):
            finish(k, r).wait_recv()
            finish(k, r).wait_send()
            spread(k, r).wait_send()
        to_pair(k, own[k]).wait_send()

        @pl.when(inner)
        def _():
            to_cross(k).wait_send()

    for r in (1, 2, 3):
        plane_copy(r).wait_send()
        line_copy(r).wait_send()
    core_copy().wait_send()


def swap_and_return(new_up, new_down, outs, partner, me):
    half, hidden_count = new_up.shape
    tok_count = outs.shape[0] // 32
    up_rows = half // (4 * UP_CHUNKS)
    down_rows = hidden_count // (4 * DOWN_CHUNKS)
    up_shape = (4, UP_CHUNKS, up_rows, hidden_count)
    down_shape = (4, DOWN_CHUNKS, down_rows, half)
    kind = new_up.dtype
    pieces = [pltpu.VMEM((4,) + up_shape[2:], kind)] * UP_CHUNKS + [
        pltpu.VMEM((4,) + down_shape[2:], kind)
    ] * DOWN_CHUNKS
    total = CHUNKS
    dma = pltpu.SemaphoreType.DMA
    block = (tok_count, half)
    by_spot = outs.reshape(4, 4, 2, tok_count, half).transpose(1, 0, 2, 3, 4)
    vmem = pl.BlockSpec(memory_space=pltpu.VMEM)
    up_end, down_end, layer = pl.pallas_call(
        swap_kernel,
        out_shape=(
            jax.ShapeDtypeStruct(up_shape, kind),
            jax.ShapeDtypeStruct(down_shape, kind),
            jax.ShapeDtypeStruct((tok_count, 2 * half), kind),
        ),
        in_specs=[pl.BlockSpec(memory_space=pltpu.SMEM), vmem, vmem, vmem],
        out_specs=(vmem, vmem, vmem),
        scratch_shapes=pieces * 6
        + [
            pltpu.VMEM((3, 4, 2) + block, kind),
            pltpu.VMEM((4, 2) + block, kind),
            pltpu.VMEM((3, 2) + block, kind),
            pltpu.VMEM((2,) + block, kind),
            pltpu.VMEM(block, kind),
            dma((total, 3)),
            dma((total, 3)),
            dma((total,)),
            dma((total,)),
            dma((total,)),
            dma((total,)),
            dma((total, 3)),
            dma((total, 3)),
            dma((3,)),
            dma((3,)),
            dma((3,)),
            dma((3,)),
            dma((1,)),
            dma((1,)),
        ],
        compiler_params=pltpu.CompilerParams(
            collective_id=1, has_side_effects=True, vmem_limit_bytes=56 * 1024 * 1024
        ),
    )(
        route_table(partner, me),
        new_up.reshape(up_shape),
        new_down.reshape(down_shape),
        by_spot,
    )
    return (
        layer,
        up_end.reshape(1, half, hidden_count),
        down_end.reshape(1, hidden_count, half),
    )


def gather_kernel(*refs):
    arrays, ends = refs[:3], refs[3:6]
    line_send, line_recv, near_send, near_recv, far_send, far_recv = refs[6:]
    me = lax.axis_index("expert")
    core = lax.axis_index("dp")
    z, spot = me // 4, me % 4
    near = [z * 4 + lax.bitwise_xor(spot, r) for r in (1, 2)]
    line = [lax.bitwise_xor(z, r) * 4 + spot for r in range(4)]
    hops = [(r, flip) for r in (0, 1, 2, 3) for flip in (0, 1) if r + flip > 0]

    barrier = pltpu.get_barrier_semaphore()
    for r, flip in hops:
        pl.semaphore_signal(
            barrier,
            inc=1,
            device_id=(line[r], lax.bitwise_xor(core, flip)),
            device_id_type=MESH,
        )
    for peer in near:
        pl.semaphore_signal(barrier, inc=1, device_id=(peer, core), device_id_type=MESH)
    pl.semaphore_wait(barrier, len(hops) + 2)

    def line_copy(a, r, flip):
        at_core = lax.bitwise_xor(core, flip)
        return pltpu.make_async_remote_copy(
            src_ref=arrays[a] if a == 2 else arrays[a].at[at_core],
            dst_ref=ends[a].at[me, core],
            send_sem=line_send.at[a, r * 2 + flip],
            recv_sem=line_recv.at[a, r * 2 + flip],
            device_id=(line[r], at_core),
            device_id_type=MESH,
        )

    def near_copy(a, r, way):
        block = ends[a].at[line[r]]
        return pltpu.make_async_remote_copy(
            src_ref=block,
            dst_ref=block,
            send_sem=near_send.at[a, r, way],
            recv_sem=near_recv.at[a, r, way],
            device_id=(near[way], core),
            device_id_type=MESH,
        )

    def far_copy(a, r):
        came = 1 if a == 1 else 0
        block = ends[a].at[lax.bitwise_xor(z, r) * 4 + lax.bitwise_xor(spot, came + 1)]
        return pltpu.make_async_remote_copy(
            src_ref=block,
            dst_ref=block,
            send_sem=far_send.at[a, r],
            recv_sem=far_recv.at[a, r],
            device_id=(near[1 - came], core),
            device_id_type=MESH,
        )

    for r, flip in hops:
        for a in range(3):
            line_copy(a, r, flip).start()
    for a in range(2):
        ends[a][me, core] = arrays[a][core]
    ends[2][me, core] = arrays[2][...]

    for step in range(5):
        if step < 4:
            for a in range(3):
                for flip in (0, 1):
                    if step + flip > 0:
                        line_copy(a, step, flip).wait_recv()
                for way in (0, 1):
                    near_copy(a, step, way).start()
        if step >= 1:
            for a in range(3):
                came = 1 if a == 1 else 0
                near_copy(a, step - 1, came).wait_recv()
                far_copy(a, step - 1).start()

    for a in range(3):
        for r in range(4):
            near_copy(a, r, 0 if a == 1 else 1).wait_recv()
            far_copy(a, r).wait_recv()
            far_copy(a, r).wait_send()
            for way in (0, 1):
                near_copy(a, r, way).wait_send()
        for r, flip in hops:
            line_copy(a, r, flip).wait_send()


def gather_tokens(tokens, cotangent, by_slot, me):
    tok_count, feature_count = tokens.shape
    half = feature_count // 2
    kind = tokens.dtype

    def by_half(array_item):
        return array_item.reshape(tok_count, 2, half).transpose(1, 0, 2)

    flat = by_slot.T.reshape(-1, 128)
    table_rows = flat.shape[0]
    flat = jnp.pad(flat, ((0, 8 - table_rows), (0, 0)))
    vmem = pl.BlockSpec(memory_space=pltpu.VMEM)
    dma = pltpu.SemaphoreType.DMA
    full = jax.ShapeDtypeStruct((16, 2, tok_count, half), kind)
    rows, cots, tables = pl.pallas_call(
        gather_kernel,
        out_shape=(full, full, jax.ShapeDtypeStruct((16, 2, 8, 128), jnp.float32)),
        in_specs=[vmem] * 3,
        out_specs=(vmem,) * 3,
        scratch_shapes=[
            dma((3, 8)),
            dma((3, 8)),
            dma((3, 4, 2)),
            dma((3, 4, 2)),
            dma((3, 4)),
            dma((3, 4)),
        ],
        compiler_params=pltpu.CompilerParams(
            collective_id=2, has_side_effects=True, vmem_limit_bytes=32 * 1024 * 1024
        ),
    )(by_half(tokens), by_half(cotangent), flat)
    weights = tables[:, :, :table_rows].reshape(32, 16, tok_count)
    hit = jnp.arange(16)[None, :, None] == me
    scale = jnp.sum(jnp.where(hit, weights, 0.0), axis=1).reshape(-1, 1)
    return rows.reshape(-1, half), cots.reshape(-1, half), scale


def dense_body(
    tokens,
    expert_ids,
    route_weight,
    cotangent,
    holder,
    partner,
    up_weight,
    down_weight,
    up_moment,
    down_moment,
):
    n_slots = lax.axis_size("expert")
    swap_pair = [(0, 1), (1, 0)]
    me = lax.axis_index("expert")
    by_slot = own_weights(expert_ids, route_weight, holder, n_slots)
    rows, cots, scale = gather_tokens(tokens, cotangent, by_slot, me)
    grads = (scale * cots.astype(jnp.float32)).astype(jnp.bfloat16)
    up_local, down_local = up_weight[0], down_weight[0]
    pre_part = jnp.dot(rows, up_local, preferred_element_type=jnp.float32).astype(jnp.bfloat16)
    back_part = lax.dot_general(
        grads, down_local, (((1,), (1,)), ((), ())), preferred_element_type=jnp.float32
    ).astype(jnp.bfloat16)
    preact = pre_part.astype(jnp.float32) + lax.ppermute(pre_part, "dp", swap_pair).astype(
        jnp.float32
    )
    back_sum = back_part.astype(jnp.float32) + lax.ppermute(back_part, "dp", swap_pair).astype(
        jnp.float32
    )
    hidden = jax.nn.silu(preact).astype(jnp.bfloat16)
    pre_grad = (back_sum * silu_slope(preact)).astype(jnp.bfloat16)
    up_grad = lax.dot_general(
        rows, pre_grad, (((0,), (0,)), ((), ())), preferred_element_type=jnp.float32
    )
    new_up = (
        MOMENT_DECAY * up_moment[0].astype(jnp.float32) + (1.0 - MOMENT_DECAY) * up_grad
    ).astype(jnp.bfloat16)
    down_grad = lax.dot_general(
        hidden, grads, (((0,), (0,)), ((), ())), preferred_element_type=jnp.float32
    )
    new_down = (
        MOMENT_DECAY * down_moment[0].astype(jnp.float32) + (1.0 - MOMENT_DECAY) * down_grad
    ).astype(jnp.bfloat16)
    out_part = jnp.dot(hidden, down_local, preferred_element_type=jnp.float32).astype(jnp.bfloat16)
    out_part = (scale * out_part.astype(jnp.float32)).astype(jnp.bfloat16)
    return swap_and_return(new_up, new_down, out_part, partner, me)


def pick_body(mesh):
    def chosen(tokens, *others):
        dense = mesh.shape["dp"] == 2 and mesh.shape["expert"] == 16
        return (dense_body if dense else body)(tokens, *others)

    return chosen


def solution(mesh):
    return jax.shard_map(
        pick_body(mesh),
        mesh=mesh,
        in_specs=(
            P(("expert", "dp"), None),
            P(("expert", "dp"), None),
            P(("expert", "dp"), None),
            P(("expert", "dp"), None),
            P(),
            P(),
            P("expert", "dp", None),
            P("expert", None, "dp"),
            P("expert", "dp", None),
            P("expert", None, "dp"),
        ),
        out_specs=(P(("expert", "dp"), None), P("expert", "dp", None), P("expert", None, "dp")),
        check_vma=False,
    )
```
